32 devices in a mesh: parts: 2 (over y), group: 4 (over x, core), member: 4 (over z), half: 1.
Axes of the slice: x: 2, y: 2, z: 4, core: 2. Of those that a mesh axis runs over, the one named last changes fastest.
Arguments:
- tokens: bfloat16 [2048, 1344], P(('parts', 'group', 'member'), 'half'), parts along dimension 0, may hold values from -120 to 120
- norm_gain: float32 [1344], replicated, may hold values from 0.25 to 1.75
- w_up: bfloat16 [16, 1344, 928], P(('group', 'member'), None, 'half'), may hold values from -0.15625 to 0.15625
- w_down: bfloat16 [16, 928, 1344], P(('group', 'member'), 'half'), may hold values from -0.1875 to 0.1875
- expert_ids: int32 [2048, 6], P(('parts', 'group', 'member')), parts along dimension 0, may hold values from 0 to 15, all different within a row; in each aligned block of 32 rows (0 to 31, 32 to 63, ...) at most 24 rows name the same one
- gates: float32 [2048, 6], P(('parts', 'group', 'member')), parts along dimension 0, may hold values from 0.05 to 0.4
Outputs:
- mixed: bfloat16 [2048, 1344], P(('parts', 'group', 'member'), 'half'), parts along dimension 0
The draws below stay inside these ranges and needn't reach their ends.
There are 2 independent parts, one for each index of `parts`. The reference program is written for one: setup_inputs(seed, part) draws one part's arguments, and reference() takes and returns one part's arrays. A program takes and returns all parts, laid end to end along the dimension named above; an argument that names none is the same for every part. Nothing has to cross between parts.
Inputs may be any that keep to these rules, and one draw needn't show every extreme that they name: `expert_ids`: each token names 6 different experts; in each aligned block of 32 tokens no expert is named by more than 24 tokens, and in some blocks one is named by exactly 24.
All inputs are finite; a program needn't handle non-finite values.
Results may differ from the reference program's by a relative error of at most 0.0073.
Values may be sent and summed in bfloat16 or wider, within the bound.
A program may use at most 64 MiB of HBM per device.

```python
import math
import jax
import jax.numpy as jnp
import numpy as np
from jax import lax

D = 1344
FF = 928
TOP = 6
MB_TOK = 32
EXPERTS = 16
CAP = 24
TOKENS = 1024
N_HALF = 1


def draw_tokens(key, part):
    base_key, column_key, row_key = jax.random.split(key, 3)
    column_scale = jnp.exp(jax.random.uniform(column_key, (D,), jnp.float32, 0.0, math.log(10.0)))
    row_scale = jnp.exp(jax.random.uniform(row_key, (TOKENS, 1), jnp.float32, math.log(0.5), math.log(3.0)))
    base = jnp.clip(jax.random.normal(base_key, (TOKENS, D), jnp.float32), -4.0, 4.0)
    return (base * column_scale * row_scale).astype(jnp.bfloat16)


def block_levels(rng, dims, shards, low, high):
    def one(dim, parts):
        steps = jax.random.uniform(jax.random.fold_in(jax.random.fold_in(rng, 6), dim), (parts,), jnp.float32, low / len(shards), high / len(shards))
        return jnp.repeat(jnp.exp(steps), dims[dim] // parts).reshape((-1,) + (1,) * (len(dims) - dim - 1))

    loudness = one(*shards[0])
    for cut in shards[1:]:
        loudness = loudness * one(*cut)
    return loudness


def deal_out(rng, own, number, rows, number_of, top, bound, slope):
    ranking = jax.random.permutation(rng, number_of)
    crowded, ordinary = shares(number_of, rows * top, bound, slope, True), shares(number_of, rows * top, bound, slope, False)
    places = jnp.arange(number_of)

    def named(lengths, rotation):
        used = int((lengths > 0).sum())
        fixed = max(1, used // 4)
        passed = fixed + (places - fixed + rotation * (used - fixed)) % max(1, number_of - fixed)
        return jnp.zeros((number_of,), jnp.int32).at[ranking[jnp.where(places < fixed, places, passed)]].set(jnp.asarray(lengths, jnp.int32))

    lengths = jnp.where(number % 4 == 0, named(crowded, number // 4), named(ordinary, number - number // 4 - 1))
    mixed = jax.random.permutation(jax.random.fold_in(own, 3), number_of)
    giver, sink = mixed[0:number_of // 2 * 2:2], mixed[1:number_of // 2 * 2:2]
    margin = jnp.minimum(lengths[giver] - 1, bound - lengths[sink]) // 2
    margin = jnp.where((giver == ranking[0]) | (sink == ranking[0]) | (lengths[sink] == 0), 0, jnp.maximum(margin, 0))
    passed = jax.random.randint(jax.random.fold_in(own, 4), (number_of // 2,), 0, 1 << 20) % (margin + 1)
    lengths = lengths.at[giver].add(-passed).at[sink].add(passed)
    items = jnp.searchsorted(jnp.cumsum(lengths), jnp.arange(rows * top), side="right").astype(jnp.int32)
    listing = items.reshape(top, rows).T
    listing = listing[jax.random.permutation(jax.random.fold_in(own, 1), rows)]
    rotation = jax.random.randint(jax.random.fold_in(own, 2), (rows, 1), 0, top)
    return jnp.take_along_axis(listing, (jnp.arange(top)[None, :] + rotation) % top, axis=1)


def shares(number_of, total, bound, lean, full):
    weights = [(1 << 20) // math.isqrt(grade ** lean) + 1 for grade in range(1, number_of + 1)]
    largest = bound if full else min(bound, max(-(-total // number_of), total * weights[0] // sum(weights)))
    least = 1 if total - largest >= number_of - 1 else 0
    given, surplus = [largest] + [least] * (number_of - 1), total - largest - least * (number_of - 1)
    while surplus > 0:
        movable = [i for i in range(1, number_of) if given[i] < largest] or [i for i in range(1, number_of) if given[i] < bound]
        whole, remaining = sum([weights[i] for i in movable]), surplus
        for i in movable:
            extra = min(bound - given[i], max(1, remaining * weights[i] // whole), surplus)
            given[i] = given[i] + extra
            surplus = surplus - extra
    return np.array(given)


def noise(own_key, extent, scale, limit, shards=(), kind=jnp.bfloat16):
    entries = jax.random.normal(own_key, extent, jnp.float32) * scale
    if len(shards) > 0:
        entries = block_levels(own_key, extent, shards, -0.22, 0.18) * entries
    return jnp.clip(entries, min=-limit, max=limit).astype(kind)


def setup_inputs(seed: int = 0, part: int = 0) -> dict:
    key_list = jax.random.split(jax.random.key(seed), 7)
    part_keys = jax.random.split(jax.random.fold_in(key_list[6], part), 7)
    tokens = draw_tokens(jax.random.fold_in(jax.random.fold_in(key_list[6], part), 71), part)
    norm_gain = jnp.clip(1.0 + 0.15 * jax.random.normal(key_list[1], (D,), jnp.float32), 0.25, 1.75)
    w_up = noise(key_list[2], (EXPERTS, D, FF), D ** -0.5, 0.15625, ((0, 16),))
    w_down = noise(key_list[3], (EXPERTS, FF, D), FF ** -0.5, 0.1875, ((0, 16),))
    expert_ids_keys = jax.random.split(jax.random.fold_in(part_keys[4], 1), TOKENS // MB_TOK)
    expert_ids_turns = jax.random.permutation(jax.random.fold_in(part_keys[4], 3), TOKENS // MB_TOK)
    expert_ids = jax.vmap(lambda own, number: deal_out(jax.random.fold_in(part_keys[4], 2), own, number, MB_TOK, EXPERTS, TOP, CAP, 2))(expert_ids_keys, expert_ids_turns).reshape((TOKENS, TOP))
    gates = jnp.clip(0.05 + 0.35 * jax.random.uniform(part_keys[5], (TOKENS, TOP), jnp.float32) ** block_levels(part_keys[5], (TOKENS, TOP), ((0, 16),), -0.2, 0.2), 0.05, 0.4)
    return {"tokens": tokens, "norm_gain": norm_gain, "w_up": w_up, "w_down": w_down, "expert_ids": expert_ids, "gates": gates}


epsilon = 1e-05

def reference(tokens, norm_gain, w_up, w_down, expert_ids, gates):
    values = tokens.astype(jnp.float32)
    mean_square = lax.optimization_barrier(jnp.mean(values * values, axis=-1, keepdims=True))
    normed = (values * lax.rsqrt(mean_square + epsilon) * norm_gain).astype(jnp.bfloat16)
    tokens_total = normed.shape[0]
    width = normed.shape[1]
    hidden_units = w_up.shape[2]
    most_rows = tokens_total // MB_TOK * CAP

    def one_expert(accumulated, expert):
        matches = expert_ids == expert
        weight = lax.optimization_barrier(jnp.sum(jnp.where(matches, gates, jnp.float32(0.0)), axis=1))
        chosen = jnp.any(matches, axis=1)
        positions = jnp.nonzero(chosen, size=most_rows, fill_value=0)[0].astype(jnp.int32)
        filled = jnp.arange(most_rows, dtype=jnp.int32) < jnp.sum(chosen.astype(jnp.int32))
        routed = normed[positions]
        up_values = jnp.dot(routed, w_up[expert], preferred_element_type=jnp.float32)
        hidden = jnp.square(jax.nn.relu(up_values)).astype(jnp.bfloat16)
        hidden_parts = hidden.reshape(most_rows, N_HALF, hidden_units // N_HALF).astype(jnp.float32)
        down_parts = w_down[expert].reshape(N_HALF, hidden_units // N_HALF, width).astype(jnp.float32)
        partial_value = jnp.einsum('rhf,hfd->hrd', hidden_parts, down_parts)
        rounded = lax.optimization_barrier(partial_value.astype(jnp.bfloat16)).astype(jnp.float32)
        expert_out = lax.optimization_barrier(lax.optimization_barrier(jnp.sum(rounded, axis=0)).astype(jnp.bfloat16)).astype(jnp.float32)
        contrib = jnp.where(filled, weight[positions], jnp.float32(0.0))[:, None] * expert_out
        return (accumulated.at[positions].add(contrib), None)
    start_sum = jnp.zeros((tokens_total, width), jnp.float32)
    total_sum, _ = lax.scan(one_expert, start_sum, jnp.arange(w_up.shape[0], dtype=jnp.int32))
    return total_sum.astype(jnp.bfloat16)
```

```python
import functools

import jax
import jax.numpy as jnp
from jax import lax
from jax.experimental import pallas as pl
from jax.experimental.pallas import tpu as pltpu
from jax.sharding import PartitionSpec as P

MB_TOK = 32
LANES = 128

epsilon = 1e-05


def visiting_orders(members):
    middle = (members - 1) / 2
    return [
        sorted(range(members), key=lambda s: (abs(s - m), abs(s - middle)))
        for m in range(members)
    ]


def fused_kernel(
    members,
    tok_ref,
    gain_ref,
    ids_ref,
    gates_ref,
    up_hbm,
    down_hbm,
    out_ref,
    gathered,
    up_ref,
    down_ref,
    partials,
    core_in,
    core_sum,
    x_in,
    chain_out,
    chain_in,
    w_sem,
    ag_send,
    ag_recv,
    own_send,
    core_send,
    core_recv,
    x_send,
    x_recv,
    chain_send,
    chain_recv,
):
    rows, width = tok_ref.shape
    picks = ids_ref.shape[1]
    padded = gathered.shape[2]
    base = width // LANES * LANES
    off = width - base
    part = lax.axis_index("parts")
    g = lax.axis_index("group")
    m = lax.axis_index("member")
    half = lax.axis_index("half")
    experts = lax.axis_size("group") * members
    me = g * members + m
    core_peer = (part, g + 1 - 2 * lax.rem(g, 2), m, half)
    x_peer = (part, lax.rem(g + 2, 4), m, half)
    has_left = m > 0
    has_right = m < members - 1

    def chain_peer(place):
        return (part, g, place, half)

    up_copy = pltpu.make_async_copy(up_hbm.at[0], up_ref.at[pl.ds(0, width), :], w_sem.at[0])
    down_copy = pltpu.make_async_copy(down_hbm.at[0], down_ref, w_sem.at[1])
    up_copy.start()
    down_copy.start()

    barrier = pltpu.get_barrier_semaphore()

    def greet(peer):
        pl.semaphore_signal(barrier, inc=1, device_id=peer, device_id_type=pl.DeviceIdType.MESH)

    greet(core_peer)
    greet(x_peer)

    @pl.when(has_left)
    def _():
        greet(chain_peer(m - 1))

    @pl.when(has_right)
    def _():
        greet(chain_peer(m + 1))

    block = padded - base
    lane = lax.broadcasted_iota(jnp.int32, (rows, block), 1) - off
    piece = (lane >= experts).astype(jnp.int32) + (lane >= 2 * experts).astype(jnp.int32)
    lane_expert = lane - piece * experts
    weight = jnp.zeros((rows, block), jnp.float32)
    for k in range(picks):
        weight += jnp.where(lane_expert == ids_ref[:, k : k + 1], gates_ref[:, k : k + 1], 0.0)
    high = weight.astype(jnp.bfloat16).astype(jnp.float32)
    rest = weight - high
    middle = rest.astype(jnp.bfloat16).astype(jnp.float32)
    low = rest - middle
    pieces = jnp.where(piece == 0, high, jnp.where(piece == 1, middle, low))
    values = tok_ref[...].astype(jnp.float32)
    inverse_rms = lax.rsqrt(jnp.mean(values * values, axis=-1, keepdims=True) + epsilon)
    normed = (values * inverse_rms * gain_ref[...]).astype(jnp.bfloat16)
    own_rows = pl.ds(0, rows)
    gathered[m, own_rows, base:padded] = jnp.zeros((rows, block), jnp.bfloat16)
    gathered[m, own_rows, 0:width] = normed
    tail = gathered[m, own_rows, base:padded].astype(jnp.float32)
    gathered[m, own_rows, base:padded] = jnp.where(lane < 0, tail, pieces).astype(jnp.bfloat16)
    up_ref[pl.ds(width, padded - width), :] = jnp.zeros((padded - width, up_ref.shape[1]), jnp.bfloat16)

    pl.semaphore_wait(barrier, 2 + has_left.astype(jnp.int32) + has_right.astype(jnp.int32))

    def gather_copy(s, source, target, peer, send):
        return pltpu.make_async_remote_copy(
            src_ref=gathered.at[s, pl.ds(source * rows, rows), :],
            dst_ref=gathered.at[s, pl.ds(target * rows, rows), :],
            send_sem=send,
            recv_sem=ag_recv.at[target, s],
            device_id=peer,
            device_id_type=pl.DeviceIdType.MESH,
        )

    def to_chain(s, place):
        return gather_copy(s, 0, 0, chain_peer(place), ag_send.at[0, s])

    def to_left_first():
        return gather_copy(m, 0, 0, chain_peer(m - 1), own_send.at[0])

    def to_right_first():
        return gather_copy(m, 0, 0, chain_peer(m + 1), own_send.at[1])

    def to_x(s):
        return gather_copy(s, 0, 1, x_peer, ag_send.at[1, s])

    def to_core(s):
        return gather_copy(s, 0, 2, core_peer, ag_send.at[2, s])

    def to_core_far(s):
        return gather_copy(s, 1, 3, core_peer, ag_send.at[3, s])

    @pl.when(has_left)
    def _():
        to_left_first().start()

    @pl.when(has_right)
    def _():
        to_right_first().start()

    to_x(m).start()
    to_core(m).start()

    orders = visiting_orders(members)

    def place_at(i):
        code = m * members + i
        found = jnp.int32(0)
        for a in range(members):
            for b in range(members):
                found = found + jnp.where(code == a * members + b, orders[a][b], 0)
        return found

    def pass_on(s, next_place, goes_on):
        to_chain(s, next_place).wait_recv()

        @pl.when(goes_on)
        def _():
            to_chain(s, next_place).start()

        to_x(s).start()
        to_core(s).start()

    def core_copy(s):
        return pltpu.make_async_remote_copy(
            src_ref=partials.at[s, pl.ds(2 * rows, 2 * rows), :],
            dst_ref=core_in.at[s],
            send_sem=core_send.at[s],
            recv_sem=core_recv.at[s],
            device_id=core_peer,
            device_id_type=pl.DeviceIdType.MESH,
        )

    def x_copy(s):
        return pltpu.make_async_remote_copy(
            src_ref=core_sum.at[s, pl.ds(rows, rows), :],
            dst_ref=x_in.at[s],
            send_sem=x_send.at[s],
            recv_sem=x_recv.at[s],
            device_id=x_peer,
            device_id_type=pl.DeviceIdType.MESH,
        )

    def chain_copy(s, side, place):
        return pltpu.make_async_remote_copy(
            src_ref=chain_out.at[s],
            dst_ref=chain_in.at[side, s],
            send_sem=chain_send.at[s],
            recv_sem=chain_recv.at[side, s],
            device_id=chain_peer(place),
            device_id_type=pl.DeviceIdType.MESH,
        )

    all_lane = lax.broadcasted_iota(jnp.int32, (4 * rows, block), 1) - off
    mine = (all_lane == me) | (all_lane == me + experts) | (all_lane == me + 2 * experts)

    def gather_step(i, carry):
        left = m - i - 1
        right = m + i + 1

        @pl.when(left >= 0)
        def _():
            pass_on(left, m + 1, has_right)

        @pl.when(right < members)
        def _():
            pass_on(right, m - 1, has_left)

        s = place_at(i)
        to_x(s).wait_recv()
        to_core_far(s).start()
        to_core(s).wait_recv()
        to_core_far(s).wait_recv()

        @pl.when(i == 0)
        def _():
            up_copy.wait()
            down_copy.wait()

        tail_block = gathered[s, :, base:padded].astype(jnp.float32)
        row_weight = jnp.sum(jnp.where(mine, tail_block, 0.0), axis=1, keepdims=True)
        up_values = jnp.dot(gathered[s], up_ref[...], preferred_element_type=jnp.float32)
        hidden = jnp.square(jnp.maximum(up_values, 0.0)).astype(jnp.bfloat16)
        down_values = jnp.dot(hidden, down_ref[...], preferred_element_type=jnp.float32)
        partials[s] = (down_values * row_weight).astype(jnp.bfloat16)
        core_copy(s).start()
        return carry

    lax.fori_loop(0, members, gather_step, 0)

    def add(a, b):
        return a.astype(jnp.float32) + b.astype(jnp.float32)

    def core_step(i, carry):
        s = place_at(members - 1 - i)
        core_copy(s).wait_recv()
        far = pl.ds(rows, rows)
        core_sum[s, far, :] = add(partials[s, far, :], core_in[s, far, :]).astype(jnp.bfloat16)
        x_copy(s).start()
        return carry

    lax.fori_loop(0, members, core_step, 0)

    def own_sum(s):
        x_copy(s).wait_recv()
        return add(partials[s, own_rows, :], core_in[s, own_rows, :]) + x_in[s].astype(jnp.float32)

    def chain_step(i, carry):
        s = place_at(members - 1 - i)
        total = own_sum(s)

        def onward(side, upstream, next_place):
            @pl.when(upstream)
            def _():
                chain_copy(s, side, next_place).wait_recv()
                chain_out[s] = (total + chain_in[side, s].astype(jnp.float32)).astype(jnp.bfloat16)

            @pl.when(jnp.logical_not(upstream))
            def _():
                chain_out[s] = total.astype(jnp.bfloat16)

            chain_copy(s, side, next_place).start()

        @pl.when(s > m)
        def _():
            onward(0, has_left, m + 1)

        @pl.when(s < m)
        def _():
            onward(1, has_right, m - 1)

        return carry

    lax.fori_loop(0, members - 1, chain_step, 0)

    total = own_sum(m)

    @pl.when(has_left & has_right)
    def _():
        chain_copy(m, 0, m + 1).wait_recv()
        chain_copy(m, 1, m - 1).wait_recv()
        both = add(chain_in[0, m], chain_in[1, m])
        out_ref[...] = (total + both).astype(out_ref.dtype)

    @pl.when(has_left & jnp.logical_not(has_right))
    def _():
        chain_copy(m, 0, m - 1).wait_recv()
        out_ref[...] = (total + chain_in[0, m].astype(jnp.float32)).astype(out_ref.dtype)

    @pl.when(has_right & jnp.logical_not(has_left))
    def _():
        chain_copy(m, 1, m + 1).wait_recv()
        out_ref[...] = (total + chain_in[1, m].astype(jnp.float32)).astype(out_ref.dtype)

    @pl.when(has_left)
    def _():
        to_left_first().wait_send()

    @pl.when(has_right)
    def _():
        to_right_first().wait_send()

    def finish(s, carry):
        to_x(s).wait_send()
        to_core(s).wait_send()
        to_core_far(s).wait_send()
        core_copy(s).wait_send()
        x_copy(s).wait_send()

        @pl.when((s < m) & has_right)
        def _():
            to_chain(s, m + 1).wait_send()

        @pl.when((s > m) & has_left)
        def _():
            to_chain(s, m - 1).wait_send()

        @pl.when(s > m)
        def _():
            chain_copy(s, 0, m + 1).wait_send()

        @pl.when(s < m)
        def _():
            chain_copy(s, 1, m - 1).wait_send()

        return carry

    lax.fori_loop(0, members, finish, 0)


def fused_on_device(tokens, norm_gain, w_up, w_down, expert_ids, gates):
    members = lax.axis_size("member")
    experts = lax.axis_size("group") * members
    rows, width = tokens.shape
    hidden_width = w_up.shape[2]
    padded = -(-(width + 3 * experts) // LANES) * LANES
    vmem = pl.BlockSpec(memory_space=pltpu.VMEM)
    hbm = pl.BlockSpec(memory_space=pl.ANY)
    dma = pltpu.SemaphoreType.DMA
    total_rows = 4 * members * rows
    return pl.pallas_call(
        functools.partial(fused_kernel, members),
        out_shape=jax.ShapeDtypeStruct((rows, width), jnp.bfloat16),
        in_specs=[vmem, vmem, vmem, vmem, hbm, hbm],
        out_specs=vmem,
        scratch_shapes=[
            pltpu.VMEM((members, 4 * rows, padded), jnp.bfloat16),
            pltpu.VMEM((padded, hidden_width), jnp.bfloat16),
            pltpu.VMEM((hidden_width, width), jnp.bfloat16),
            pltpu.VMEM((members, 4 * rows, width), jnp.bfloat16),
            pltpu.VMEM((members, 2 * rows, width), jnp.bfloat16),
            pltpu.VMEM((members, 2 * rows, width), jnp.bfloat16),
            pltpu.VMEM((members, rows, width), jnp.bfloat16),
            pltpu.VMEM((members, rows, width), jnp.bfloat16),
            pltpu.VMEM((2, members, rows, width), jnp.bfloat16),
            dma((2,)),
            dma((4, members)),
            dma((4, members)),
            dma((2,)),
            dma((members,)),
            dma((members,)),
            dma((members,)),
            dma((members,)),
            dma((members,)),
            dma((2, members)),
        ],
        compiler_params=pltpu.CompilerParams(
            collective_id=0, has_side_effects=True, vmem_limit_bytes=48 * 2**20
        ),
        cost_estimate=pl.CostEstimate(
            flops=4 * total_rows * width * hidden_width,
            bytes_accessed=4 * width * hidden_width,
            transcendentals=0,
        ),
    )(tokens, norm_gain.reshape(1, width), expert_ids, gates, w_up, w_down)


def routed_on_device(tokens, norm_gain, w_up, w_down, expert_ids, gates):
    groups = lax.axis_size("group")
    members = lax.axis_size("member")
    experts = groups * members
    tok_dev, picks = expert_ids.shape
    block_rows = MB_TOK
    capacity = min(block_rows, (2 * picks * block_rows + experts - 1) // experts)
    micro_count = tok_dev // block_rows
    half_width = tokens.shape[1]
    up_local = w_up[0]
    down_local = w_down[0]
    full_rows = lax.all_gather(tokens, "half", axis=1, tiled=True)
    full_float = full_rows.astype(jnp.float32)
    inverse_rms = lax.rsqrt(jnp.mean(full_float * full_float, axis=-1, keepdims=True) + epsilon)
    normed = (full_float * inverse_rms * norm_gain).astype(jnp.bfloat16)
    token_blocks = normed.reshape(micro_count, block_rows, normed.shape[1])
    id_blocks = expert_ids.reshape(micro_count, block_rows, picks)
    gate_blocks = gates.reshape(micro_count, block_rows, picks)
    row_iota = jnp.arange(block_rows, dtype=jnp.int32)
    earlier = (row_iota[:, None] > row_iota[None, :]).astype(jnp.bfloat16)

    def one_block(pieces):
        block_tokens, block_ids, weights = pieces
        expert_iota = jnp.arange(experts, dtype=jnp.int32)
        matches = block_ids[:, :, None] == expert_iota[None, None, :]
        picked = jnp.any(matches, axis=1)
        before = jnp.dot(
            earlier, picked.astype(jnp.bfloat16), preferred_element_type=jnp.float32
        ).astype(jnp.int32)
        slot_iota = jnp.arange(capacity, dtype=jnp.int32)
        slot_table = picked[:, :, None] & (before[:, :, None] == slot_iota[None, None, :])
        slot_bf = slot_table.astype(jnp.bfloat16).reshape(block_rows, experts * capacity)
        outgoing = lax.dot_general(
            slot_bf, block_tokens, (((0,), (0,)), ((), ())), preferred_element_type=jnp.float32
        )
        outgoing = outgoing.astype(jnp.bfloat16).reshape(experts, capacity, block_tokens.shape[1])
        arrived = lax.all_to_all(
            outgoing, ("group", "member"), split_axis=0, concat_axis=0, tiled=True
        )
        flat_rows = arrived.reshape(experts * capacity, arrived.shape[2])
        up_values = jnp.dot(flat_rows, up_local, preferred_element_type=jnp.float32)
        hidden = jnp.square(jax.nn.relu(up_values)).astype(jnp.bfloat16)
        partial_value = jnp.dot(hidden, down_local, preferred_element_type=jnp.float32).astype(
            jnp.bfloat16
        )
        partial_value = lax.optimization_barrier(partial_value).astype(jnp.float32)
        summed = lax.psum_scatter(
            partial_value.astype(jnp.bfloat16), "half", scatter_dimension=1, tiled=True
        )
        results = summed.reshape(experts, capacity, half_width)
        returned = lax.all_to_all(
            results, ("group", "member"), split_axis=0, concat_axis=0, tiled=True
        )
        select_table = (matches[:, :, :, None] & slot_table[:, None, :, :]).astype(jnp.bfloat16)
        select_table = select_table.reshape(block_rows, picks, experts * capacity)
        chosen_rows = jnp.einsum(
            "tks,sd->tkd",
            select_table,
            returned.reshape(experts * capacity, half_width),
            preferred_element_type=jnp.float32,
        )
        block_out = jnp.sum(weights[:, :, None] * chosen_rows, axis=1)
        return block_out.astype(jnp.bfloat16)

    outputs = lax.map(one_block, (token_blocks, id_blocks, gate_blocks))
    return outputs.reshape(tok_dev, half_width)


def solution(mesh):
    in_specs = (
        P(("parts", "group", "member"), "half"),
        P(),
        P(("group", "member"), None, "half"),
        P(("group", "member"), "half", None),
        P(("parts", "group", "member"), None),
        P(("parts", "group", "member"), None),
    )
    out_specs = P(("parts", "group", "member"), "half")
    fused = mesh.shape["half"] == 1 and mesh.shape["group"] == 4 and 1 < mesh.shape["member"] <= 4
    on_device = fused_on_device if fused else routed_on_device
    return jax.shard_map(
        on_device, mesh=mesh, in_specs=in_specs, out_specs=out_specs, check_vma=False
    )
```

```python
import functools

import jax
import jax.numpy as jnp
from jax import lax
from jax.experimental import pallas as pl
from jax.experimental.pallas import tpu as pltpu
from jax.sharding import PartitionSpec as P

MB_TOK = 32
LANES = 128

epsilon = 1e-05


def visiting_orders(members):
    middle = (members - 1) / 2
    return [
        sorted(range(members), key=lambda s: (abs(s - m), abs(s - middle)))
        for m in range(members)
    ]


def fused_kernel(
    members,
    tok_ref,
    gain_ref,
    ids_ref,
    gates_ref,
    up_hbm,
    down_hbm,
    out_ref,
    gathered,
    up_ref,
    down_ref,
    partials,
    core_in,
    core_sum,
    x_in,
    chain_out,
    chain_in,
    w_sem,
    ag_send,
    ag_recv,
    own_send,
    core_send,
    core_recv,
    x_send,
    x_recv,
    chain_send,
    chain_recv,
):
    rows, width = tok_ref.shape
    picks = ids_ref.shape[0]
    padded = gathered.shape[2]
    base = width // LANES * LANES
    off = width - base
    part = lax.axis_index("parts")
    g = lax.axis_index("group")
    m = lax.axis_index("member")
    half = lax.axis_index("half")
    experts = lax.axis_size("group") * members
    me = g * members + m
    core_peer = (part, g + 1 - 2 * lax.rem(g, 2), m, half)
    x_peer = (part, lax.rem(g + 2, 4), m, half)
    has_left = m > 0
    has_right = m < members - 1

    def chain_peer(place):
        return (part, g, place, half)

    up_copy = pltpu.make_async_copy(up_hbm.at[0], up_ref, w_sem.at[0])
    down_copy = pltpu.make_async_copy(down_hbm.at[0], down_ref, w_sem.at[1])
    up_copy.start()
    down_copy.start()

    barrier = pltpu.get_barrier_semaphore()

    def greet(peer):
        pl.semaphore_signal(barrier, inc=1, device_id=peer, device_id_type=pl.DeviceIdType.MESH)

    greet(core_peer)
    greet(x_peer)

    @pl.when(has_left)
    def _():
        greet(chain_peer(m - 1))

    @pl.when(has_right)
    def _():
        greet(chain_peer(m + 1))

    block = padded - base
    spot = lax.broadcasted_iota(jnp.int32, (block, rows), 0) - off
    piece = (spot >= experts).astype(jnp.int32) + (spot >= 2 * experts).astype(jnp.int32)
    spot_expert = spot - piece * experts
    weight = jnp.zeros((block, rows), jnp.float32)
    for k in range(picks):
        weight += jnp.where(spot_expert == ids_ref[k : k + 1, :], gates_ref[k : k + 1, :], 0.0)
    high = weight.astype(jnp.bfloat16).astype(jnp.float32)
    rest = weight - high
    middle = rest.astype(jnp.bfloat16).astype(jnp.float32)
    low = rest - middle
    pieces = jnp.where(piece == 0, high, jnp.where(piece == 1, middle, low)).T
    lane = lax.broadcasted_iota(jnp.int32, (rows, block), 1) - off
    values = tok_ref[...].astype(jnp.float32)
    inverse_rms = lax.rsqrt(jnp.mean(values * values, axis=-1, keepdims=True) + epsilon)
    normed = (values * inverse_rms * gain_ref[...].reshape(1, width)).astype(jnp.bfloat16)
    own_rows = pl.ds(0, rows)
    gathered[m, own_rows, base:padded] = jnp.zeros((rows, block), jnp.bfloat16)
    gathered[m, own_rows, 0:width] = normed
    tail = gathered[m, own_rows, base:padded].astype(jnp.float32)
    gathered[m, own_rows, base:padded] = jnp.where(lane < 0, tail, pieces).astype(jnp.bfloat16)

    pl.semaphore_wait(barrier, 2 + has_left.astype(jnp.int32) + has_right.astype(jnp.int32))

    def gather_copy(s, source, target, peer, send):
        return pltpu.make_async_remote_copy(
            src_ref=gathered.at[s, pl.ds(source * rows, rows), :],
            dst_ref=gathered.at[s, pl.ds(target * rows, rows), :],
            send_sem=send,
            recv_sem=ag_recv.at[target, s],
            device_id=peer,
            device_id_type=pl.DeviceIdType.MESH,
        )

    def to_chain(s, place):
        return gather_copy(s, 0, 0, chain_peer(place), ag_send.at[0, s])

    def to_left_first():
        return gather_copy(m, 0, 0, chain_peer(m - 1), own_send.at[0])

    def to_right_first():
        return gather_copy(m, 0, 0, chain_peer(m + 1), own_send.at[1])

    def to_x(s):
        return gather_copy(s, 0, 1, x_peer, ag_send.at[1, s])

    def to_core(s):
        return gather_copy(s, 0, 2, core_peer, ag_send.at[2, s])

    def to_core_far(s):
        return gather_copy(s, 1, 3, core_peer, ag_send.at[3, s])

    @pl.when(has_left)
    def _():
        to_left_first().start()

    @pl.when(has_right)
    def _():
        to_right_first().start()

    to_x(m).start()
    to_core(m).start()

    orders = visiting_orders(members)

    def place_at(i):
        code = m * members + i
        found = jnp.int32(0)
        for a in range(members):
            for b in range(members):
                found = found + jnp.where(code == a * members + b, orders[a][b], 0)
        return found

    def pass_on(s, next_place, goes_on):
        to_chain(s, next_place).wait_recv()

        @pl.when(goes_on)
        def _():
            to_chain(s, next_place).start()

        to_x(s).start()
        to_core(s).start()

    def core_copy(s):
        return pltpu.make_async_remote_copy(
            src_ref=partials.at[s, pl.ds(2 * rows, 2 * rows), :],
            dst_ref=core_in.at[s],
            send_sem=core_send.at[s],
            recv_sem=core_recv.at[s],
            device_id=core_peer,
            device_id_type=pl.DeviceIdType.MESH,
        )

    def x_copy(s):
        return pltpu.make_async_remote_copy(
            src_ref=core_sum.at[s, pl.ds(rows, rows), :],
            dst_ref=x_in.at[s],
            send_sem=x_send.at[s],
            recv_sem=x_recv.at[s],
            device_id=x_peer,
            device_id_type=pl.DeviceIdType.MESH,
        )

    def chain_copy(s, side, place):
        return pltpu.make_async_remote_copy(
            src_ref=chain_out.at[s],
            dst_ref=chain_in.at[side, s],
            send_sem=chain_send.at[s],
            recv_sem=chain_recv.at[side, s],
            device_id=chain_peer(place),
            device_id_type=pl.DeviceIdType.MESH,
        )

    all_lane = lax.broadcasted_iota(jnp.int32, (4 * rows, block), 1) - off
    mine = (all_lane == me) | (all_lane == me + experts) | (all_lane == me + 2 * experts)

    def gather_step(i, carry):
        left = m - i - 1
        right = m + i + 1

        @pl.when(left >= 0)
        def _():
            pass_on(left, m + 1, has_right)

        @pl.when(right < members)
        def _():
            pass_on(right, m - 1, has_left)

        s = place_at(i)
        to_x(s).wait_recv()
        to_core_far(s).start()
        to_core(s).wait_recv()
        to_core_far(s).wait_recv()

        @pl.when(i == 0)
        def _():
            up_copy.wait()
            down_copy.wait()

        tail_block = gathered[s, :, base:padded].astype(jnp.float32)
        row_weight = jnp.sum(jnp.where(mine, tail_block, 0.0), axis=1, keepdims=True)
        up_values = lax.dot_general(
            gathered[s, :, 0:width],
            up_ref[...],
            (((1,), (1,)), ((), ())),
            preferred_element_type=jnp.float32,
        )
        hidden = jnp.square(jnp.maximum(up_values, 0.0)).astype(jnp.bfloat16)
        down_values = jnp.dot(hidden, down_ref[...], preferred_element_type=jnp.float32)
        partials[s] = (down_values * row_weight).astype(jnp.bfloat16)
        core_copy(s).start()
        return carry

    lax.fori_loop(0, members, gather_step, 0)

    def add(a, b):
        return a.astype(jnp.float32) + b.astype(jnp.float32)

    def core_step(i, carry):
        s = place_at(members - 1 - i)
        core_copy(s).wait_recv()
        far = pl.ds(rows, rows)
        core_sum[s, far, :] = add(partials[s, far, :], core_in[s, far, :]).astype(jnp.bfloat16)
        x_copy(s).start()
        return carry

    lax.fori_loop(0, members, core_step, 0)

    def own_sum(s):
        x_copy(s).wait_recv()
        return add(partials[s, own_rows, :], core_in[s, own_rows, :]) + x_in[s].astype(jnp.float32)

    def chain_step(i, carry):
        s = place_at(members - 1 - i)
        total = own_sum(s)

        def onward(side, upstream, next_place):
            @pl.when(upstream)
            def _():
                chain_copy(s, side, next_place).wait_recv()
                chain_out[s] = (total + chain_in[side, s].astype(jnp.float32)).astype(jnp.bfloat16)

            @pl.when(jnp.logical_not(upstream))
            def _():
                chain_out[s] = total.astype(jnp.bfloat16)

            chain_copy(s, side, next_place).start()

        @pl.when(s > m)
        def _():
            onward(0, has_left, m + 1)

        @pl.when(s < m)
        def _():
            onward(1, has_right, m - 1)

        return carry

    lax.fori_loop(0, members - 1, chain_step, 0)

    total = own_sum(m)

    @pl.when(has_left & has_right)
    def _():
        chain_copy(m, 0, m + 1).wait_recv()
        chain_copy(m, 1, m - 1).wait_recv()
        both = add(chain_in[0, m], chain_in[1, m])
        out_ref[...] = (total + both).astype(out_ref.dtype)

    @pl.when(has_left & jnp.logical_not(has_right))
    def _():
        chain_copy(m, 0, m - 1).wait_recv()
        out_ref[...] = (total + chain_in[0, m].astype(jnp.float32)).astype(out_ref.dtype)

    @pl.when(has_right & jnp.logical_not(has_left))
    def _():
        chain_copy(m, 1, m + 1).wait_recv()
        out_ref[...] = (total + chain_in[1, m].astype(jnp.float32)).astype(out_ref.dtype)

    @pl.when(has_left)
    def _():
        to_left_first().wait_send()

    @pl.when(has_right)
    def _():
        to_right_first().wait_send()

    def finish(s, carry):
        to_x(s).wait_send()
        to_core(s).wait_send()
        to_core_far(s).wait_send()
        core_copy(s).wait_send()
        x_copy(s).wait_send()

        @pl.when((s < m) & has_right)
        def _():
            to_chain(s, m + 1).wait_send()

        @pl.when((s > m) & has_left)
        def _():
            to_chain(s, m - 1).wait_send()

        @pl.when(s > m)
        def _():
            chain_copy(s, 0, m + 1).wait_send()

        @pl.when(s < m)
        def _():
            chain_copy(s, 1, m - 1).wait_send()

        return carry

    lax.fori_loop(0, members, finish, 0)


def fused_on_device(tokens, norm_gain, w_up, w_down, expert_ids, gates):
    members = lax.axis_size("member")
    experts = lax.axis_size("group") * members
    rows, width = tokens.shape
    hidden_width = w_up.shape[2]
    padded = -(-(width + 3 * experts) // LANES) * LANES
    vmem = pl.BlockSpec(memory_space=pltpu.VMEM)
    hbm = pl.BlockSpec(memory_space=pl.ANY)
    dma = pltpu.SemaphoreType.DMA
    total_rows = 4 * members * rows
    return pl.pallas_call(
        functools.partial(fused_kernel, members),
        out_shape=jax.ShapeDtypeStruct((rows, width), jnp.bfloat16),
        in_specs=[vmem, vmem, vmem, vmem, hbm, hbm],
        out_specs=vmem,
        scratch_shapes=[
            pltpu.VMEM((members, 4 * rows, padded), jnp.bfloat16),
            pltpu.VMEM((hidden_width, width), jnp.bfloat16),
            pltpu.VMEM((hidden_width, width), jnp.bfloat16),
            pltpu.VMEM((members, 4 * rows, width), jnp.bfloat16),
            pltpu.VMEM((members, 2 * rows, width), jnp.bfloat16),
            pltpu.VMEM((members, 2 * rows, width), jnp.bfloat16),
            pltpu.VMEM((members, rows, width), jnp.bfloat16),
            pltpu.VMEM((members, rows, width), jnp.bfloat16),
            pltpu.VMEM((2, members, rows, width), jnp.bfloat16),
            dma((2,)),
            dma((4, members)),
            dma((4, members)),
            dma((2,)),
            dma((members,)),
            dma((members,)),
            dma((members,)),
            dma((members,)),
            dma((members,)),
            dma((2, members)),
        ],
        compiler_params=pltpu.CompilerParams(
            collective_id=0, has_side_effects=True, vmem_limit_bytes=60 * 2**20
        ),
        cost_estimate=pl.CostEstimate(
            flops=4 * total_rows * width * hidden_width,
            bytes_accessed=4 * width * hidden_width,
            transcendentals=0,
        ),
    )(tokens, norm_gain, expert_ids.T, gates.T, jnp.swapaxes(w_up, 1, 2), w_down)


def routed_on_device(tokens, norm_gain, w_up, w_down, expert_ids, gates):
    groups = lax.axis_size("group")
    members = lax.axis_size("member")
    experts = groups * members
    tok_dev, picks = expert_ids.shape
    block_rows = MB_TOK
    capacity = min(block_rows, (2 * picks * block_rows + experts - 1) // experts)
    micro_count = tok_dev // block_rows
    half_width = tokens.shape[1]
    up_local = w_up[0]
    down_local = w_down[0]
    full_rows = lax.all_gather(tokens, "half", axis=1, tiled=True)
    full_float = full_rows.astype(jnp.float32)
    inverse_rms = lax.rsqrt(jnp.mean(full_float * full_float, axis=-1, keepdims=True) + epsilon)
    normed = (full_float * inverse_rms * norm_gain).astype(jnp.bfloat16)
    token_blocks = normed.reshape(micro_count, block_rows, normed.shape[1])
    id_blocks = expert_ids.reshape(micro_count, block_rows, picks)
    gate_blocks = gates.reshape(micro_count, block_rows, picks)
    row_iota = jnp.arange(block_rows, dtype=jnp.int32)
    earlier = (row_iota[:, None] > row_iota[None, :]).astype(jnp.bfloat16)

    def one_block(pieces):
        block_tokens, block_ids, weights = pieces
        expert_iota = jnp.arange(experts, dtype=jnp.int32)
        matches = block_ids[:, :, None] == expert_iota[None, None, :]
        picked = jnp.any(matches, axis=1)
        before = jnp.dot(
            earlier, picked.astype(jnp.bfloat16), preferred_element_type=jnp.float32
        ).astype(jnp.int32)
        slot_iota = jnp.arange(capacity, dtype=jnp.int32)
        slot_table = picked[:, :, None] & (before[:, :, None] == slot_iota[None, None, :])
        slot_bf = slot_table.astype(jnp.bfloat16).reshape(block_rows, experts * capacity)
        outgoing = lax.dot_general(
            slot_bf, block_tokens, (((0,), (0,)), ((), ())), preferred_element_type=jnp.float32
        )
        outgoing = outgoing.astype(jnp.bfloat16).reshape(experts, capacity, block_tokens.shape[1])
        arrived = lax.all_to_all(
            outgoing, ("group", "member"), split_axis=0, concat_axis=0, tiled=True
        )
        flat_rows = arrived.reshape(experts * capacity, arrived.shape[2])
        up_values = jnp.dot(flat_rows, up_local, preferred_element_type=jnp.float32)
        hidden = jnp.square(jax.nn.relu(up_values)).astype(jnp.bfloat16)
        partial_value = jnp.dot(hidden, down_local, preferred_element_type=jnp.float32).astype(
            jnp.bfloat16
        )
        partial_value = lax.optimization_barrier(partial_value).astype(jnp.float32)
        summed = lax.psum_scatter(
            partial_value.astype(jnp.bfloat16), "half", scatter_dimension=1, tiled=True
        )
        results = summed.reshape(experts, capacity, half_width)
        returned = lax.all_to_all(
            results, ("group", "member"), split_axis=0, concat_axis=0, tiled=True
        )
        select_table = (matches[:, :, :, None] & slot_table[:, None, :, :]).astype(jnp.bfloat16)
        select_table = select_table.reshape(block_rows, picks, experts * capacity)
        chosen_rows = jnp.einsum(
            "tks,sd->tkd",
            select_table,
            returned.reshape(experts * capacity, half_width),
            preferred_element_type=jnp.float32,
        )
        block_out = jnp.sum(weights[:, :, None] * chosen_rows, axis=1)
        return block_out.astype(jnp.bfloat16)

    outputs = lax.map(one_block, (token_blocks, id_blocks, gate_blocks))
    return outputs.reshape(tok_dev, half_width)


def solution(mesh):
    in_specs = (
        P(("parts", "group", "member"), "half"),
        P(),
        P(("group", "member"), None, "half"),
        P(("group", "member"), "half", None),
        P(("parts", "group", "member"), None),
        P(("parts", "group", "member"), None),
    )
    out_specs = P(("parts", "group", "member"), "half")
    fused = mesh.shape["half"] == 1 and mesh.shape["group"] == 4 and 1 < mesh.shape["member"] <= 4
    on_device = fused_on_device if fused else routed_on_device
    return jax.shard_map(
        on_device, mesh=mesh, in_specs=in_specs, out_specs=out_specs, check_vma=False
    )
```

```python
import functools

import jax
import jax.numpy as jnp
from jax import lax
from jax.experimental import pallas as pl
from jax.experimental.pallas import tpu as pltpu
from jax.sharding import PartitionSpec as P

MB_TOK = 32
LANES = 128
PIECES = 4

epsilon = 1e-05


def visiting_orders(members):
    middle = (members - 1) / 2
    return [
        sorted(range(members), key=lambda s: (abs(s - m), abs(s - middle)))
        for m in range(members)
    ]


def return_orders(members):
    crossing, onward = [], []
    for m, order in enumerate(visiting_orders(members)):
        crossing.append([order[1]] + [s for s in order[::-1] if s != order[1]])
        onward.append(crossing[-1] if m in (0, members - 1) else order[::-1])
    return crossing, onward


def fused_kernel(
    members,
    tok_ref,
    gain_ref,
    ids_ref,
    gates_ref,
    up_hbm,
    down_hbm,
    out_ref,
    gathered,
    up_ref,
    down_ref,
    partials,
    core_in,
    core_sum,
    x_in,
    chain_out,
    chain_in,
    w_sem,
    ag_send,
    ag_recv,
    own_send,
    core_send,
    core_recv,
    x_send,
    x_recv,
    chain_send,
    chain_recv,
):
    rows, width = tok_ref.shape
    picks = ids_ref.shape[0]
    padded = gathered.shape[2]
    piece_rows = rows // PIECES
    base = width // LANES * LANES
    off = width - base
    part = lax.axis_index("parts")
    g = lax.axis_index("group")
    m = lax.axis_index("member")
    half = lax.axis_index("half")
    experts = lax.axis_size("group") * members
    me = g * members + m
    core_peer = (part, g + 1 - 2 * lax.rem(g, 2), m, half)
    x_peer = (part, lax.rem(g + 2, 4), m, half)
    has_left = m > 0
    has_right = m < members - 1

    def chain_peer(place):
        return (part, g, place, half)

    up_copy = pltpu.make_async_copy(up_hbm.at[0], up_ref, w_sem.at[0])
    down_copy = pltpu.make_async_copy(down_hbm.at[0], down_ref, w_sem.at[1])
    up_copy.start()
    down_copy.start()

    barrier = pltpu.get_barrier_semaphore()

    def greet(peer):
        pl.semaphore_signal(barrier, inc=1, device_id=peer, device_id_type=pl.DeviceIdType.MESH)

    greet(core_peer)
    greet(x_peer)

    @pl.when(has_left)
    def _():
        greet(chain_peer(m - 1))

    @pl.when(has_right)
    def _():
        greet(chain_peer(m + 1))

    block = padded - base
    spot = lax.broadcasted_iota(jnp.int32, (block, rows), 0) - off
    kind = (spot >= experts).astype(jnp.int32) + (spot >= 2 * experts).astype(jnp.int32)
    spot_expert = spot - kind * experts
    weight = jnp.zeros((block, rows), jnp.float32)
    for k in range(picks):
        weight += jnp.where(spot_expert == ids_ref[k : k + 1, :], gates_ref[k : k + 1, :], 0.0)
    high = weight.astype(jnp.bfloat16).astype(jnp.float32)
    rest = weight - high
    middle = rest.astype(jnp.bfloat16).astype(jnp.float32)
    low = rest - middle
    pieces = jnp.where(kind == 0, high, jnp.where(kind == 1, middle, low)).T
    lane = lax.broadcasted_iota(jnp.int32, (rows, block), 1) - off
    values = tok_ref[...].astype(jnp.float32)
    inverse_rms = lax.rsqrt(jnp.mean(values * values, axis=-1, keepdims=True) + epsilon)
    normed = (values * inverse_rms * gain_ref[...].reshape(1, width)).astype(jnp.bfloat16)
    own_rows = pl.ds(0, rows)
    gathered[m, own_rows, base:padded] = jnp.zeros((rows, block), jnp.bfloat16)
    gathered[m, own_rows, 0:width] = normed
    tail = gathered[m, own_rows, base:padded].astype(jnp.float32)
    gathered[m, own_rows, base:padded] = jnp.where(lane < 0, tail, pieces).astype(jnp.bfloat16)

    pl.semaphore_wait(barrier, 2 + has_left.astype(jnp.int32) + has_right.astype(jnp.int32))

    def gather_copy(s, h, source, target, peer, send):
        return pltpu.make_async_remote_copy(
            src_ref=gathered.at[s, pl.ds(source * rows + h * piece_rows, piece_rows), :],
            dst_ref=gathered.at[s, pl.ds(target * rows + h * piece_rows, piece_rows), :],
            send_sem=send,
            recv_sem=ag_recv.at[target, s, h],
            device_id=peer,
            device_id_type=pl.DeviceIdType.MESH,
        )

    def to_chain(s, h, place):
        return gather_copy(s, h, 0, 0, chain_peer(place), ag_send.at[0, s, h])

    def to_left_first(h):
        return gather_copy(m, h, 0, 0, chain_peer(m - 1), own_send.at[0, h])

    def to_right_first(h):
        return gather_copy(m, h, 0, 0, chain_peer(m + 1), own_send.at[1, h])

    def to_x(s, h):
        return gather_copy(s, h, 0, 1, x_peer, ag_send.at[1, s, h])

    def to_core(s, h):
        return gather_copy(s, h, 0, 2, core_peer, ag_send.at[2, s, h])

    def to_core_far(s, h):
        return gather_copy(s, h, 1, 3, core_peer, ag_send.at[3, s, h])

    for h in range(PIECES):

        @pl.when(has_left)
        def _():
            to_left_first(h).start()

        @pl.when(has_right)
        def _():
            to_right_first(h).start()

        to_x(m, h).start()
        to_core(m, h).start()

    def looked_up(orders, i):
        code = m * members + i
        found = jnp.int32(0)
        for a in range(members):
            for b in range(members):
                found = found + jnp.where(code == a * members + b, orders[a][b], 0)
        return found

    orders = visiting_orders(members)
    crossing, onward_order = return_orders(members)

    def pass_on(s, h, next_place, goes_on):
        to_chain(s, h, next_place).wait_recv()

        @pl.when(goes_on)
        def _():
            to_chain(s, h, next_place).start()

        to_x(s, h).start()
        to_core(s, h).start()

    def core_copy(s):
        return pltpu.make_async_remote_copy(
            src_ref=partials.at[s, pl.ds(2 * rows, 2 * rows), :],
            dst_ref=core_in.at[s],
            send_sem=core_send.at[s],
            recv_sem=core_recv.at[s],
            device_id=core_peer,
            device_id_type=pl.DeviceIdType.MESH,
        )

    def piece(h):
        return pl.ds(h * piece_rows, piece_rows)

    def x_copy(s, h):
        return pltpu.make_async_remote_copy(
            src_ref=core_sum.at[s, piece(h), :],
            dst_ref=x_in.at[s, piece(h), :],
            send_sem=x_send.at[s, h],
            recv_sem=x_recv.at[s, h],
            device_id=x_peer,
            device_id_type=pl.DeviceIdType.MESH,
        )

    def chain_copy(s, h, side, place):
        return pltpu.make_async_remote_copy(
            src_ref=chain_out.at[s, piece(h), :],
            dst_ref=chain_in.at[side, s, piece(h), :],
            send_sem=chain_send.at[s, h],
            recv_sem=chain_recv.at[side, s, h],
            device_id=chain_peer(place),
            device_id_type=pl.DeviceIdType.MESH,
        )

    all_lane = lax.broadcasted_iota(jnp.int32, (4 * rows, block), 1) - off
    mine = (all_lane == me) | (all_lane == me + experts) | (all_lane == me + 2 * experts)

    def add(a, b):
        return a.astype(jnp.float32) + b.astype(jnp.float32)

    def core_step(i):
        s = looked_up(crossing, i)
        core_copy(s).wait_recv()
        for h in range(PIECES):
            far = pl.ds(rows + h * piece_rows, piece_rows)
            far_sum = add(partials[s, far, :], core_in[s, far, :])
            core_sum[s, piece(h), :] = far_sum.astype(jnp.bfloat16)
            x_copy(s, h).start()

    def gather_step(i, carry):
        left = m - i - 1
        right = m + i + 1
        for h in range(PIECES):

            @pl.when(left >= 0)
            def _():
                pass_on(left, h, m + 1, has_right)

            @pl.when(right < members)
            def _():
                pass_on(right, h, m - 1, has_left)

        s = looked_up(orders, i)
        for h in range(PIECES):
            to_x(s, h).wait_recv()
            to_core_far(s, h).start()

        @pl.when(i == members - 1)
        def _():
            core_step(0)

        for h in range(PIECES):
            to_core(s, h).wait_recv()
            to_core_far(s, h).wait_recv()

        @pl.when(i == 0)
        def _():
            up_copy.wait()
            down_copy.wait()

        tail_block = gathered[s, :, base:padded].astype(jnp.float32)
        row_weight = jnp.sum(jnp.where(mine, tail_block, 0.0), axis=1, keepdims=True)
        up_values = lax.dot_general(
            gathered[s, :, 0:width],
            up_ref[...],
            (((1,), (1,)), ((), ())),
            preferred_element_type=jnp.float32,
        )
        hidden = jnp.square(jnp.maximum(up_values, 0.0)).astype(jnp.bfloat16)
        down_values = jnp.dot(hidden, down_ref[...], preferred_element_type=jnp.float32)
        partials[s] = (down_values * row_weight).astype(jnp.bfloat16)
        core_copy(s).start()
        return carry

    lax.fori_loop(0, members, gather_step, 0)

    def later_core_step(i, carry):
        core_step(i)
        return carry

    lax.fori_loop(1, members, later_core_step, 0)

    def own_sum(s, h):
        x_copy(s, h).wait_recv()
        near = add(partials[s, piece(h), :], core_in[s, piece(h), :])
        return near + x_in[s, piece(h), :].astype(jnp.float32)

    def chain_step(i, carry):
        s = looked_up(onward_order, i)

        def onward(side, upstream, next_place):
            for h in range(PIECES):
                total = own_sum(s, h)

                @pl.when(upstream)
                def _():
                    chain_copy(s, h, side, next_place).wait_recv()
                    arrived = chain_in[side, s, piece(h), :].astype(jnp.float32)
                    chain_out[s, piece(h), :] = (total + arrived).astype(jnp.bfloat16)

                @pl.when(jnp.logical_not(upstream))
                def _():
                    chain_out[s, piece(h), :] = total.astype(jnp.bfloat16)

                chain_copy(s, h, side, next_place).start()

        @pl.when(s > m)
        def _():
            onward(0, has_left, m + 1)

        @pl.when(s < m)
        def _():
            onward(1, has_right, m - 1)

        return carry

    lax.fori_loop(0, members - 1, chain_step, 0)

    for h in range(PIECES):
        total = own_sum(m, h)

        @pl.when(has_left & has_right)
        def _():
            chain_copy(m, h, 0, m + 1).wait_recv()
            chain_copy(m, h, 1, m - 1).wait_recv()
            both = add(chain_in[0, m, piece(h), :], chain_in[1, m, piece(h), :])
            out_ref[piece(h), :] = (total + both).astype(out_ref.dtype)

        @pl.when(has_left & jnp.logical_not(has_right))
        def _():
            chain_copy(m, h, 0, m - 1).wait_recv()
            one = chain_in[0, m, piece(h), :].astype(jnp.float32)
            out_ref[piece(h), :] = (total + one).astype(out_ref.dtype)

        @pl.when(has_right & jnp.logical_not(has_left))
        def _():
            chain_copy(m, h, 1, m + 1).wait_recv()
            one = chain_in[1, m, piece(h), :].astype(jnp.float32)
            out_ref[piece(h), :] = (total + one).astype(out_ref.dtype)

    for h in range(PIECES):

        @pl.when(has_left)
        def _():
            to_left_first(h).wait_send()

        @pl.when(has_right)
        def _():
            to_right_first(h).wait_send()

    def finish(s, carry):
        core_copy(s).wait_send()
        for h in range(PIECES):
            to_x(s, h).wait_send()
            to_core(s, h).wait_send()
            to_core_far(s, h).wait_send()
            x_copy(s, h).wait_send()

            @pl.when((s < m) & has_right)
            def _():
                to_chain(s, h, m + 1).wait_send()

            @pl.when((s > m) & has_left)
            def _():
                to_chain(s, h, m - 1).wait_send()

            @pl.when(s > m)
            def _():
                chain_copy(s, h, 0, m + 1).wait_send()

            @pl.when(s < m)
            def _():
                chain_copy(s, h, 1, m - 1).wait_send()

        return carry

    lax.fori_loop(0, members, finish, 0)


def fused_on_device(tokens, norm_gain, w_up, w_down, expert_ids, gates):
    members = lax.axis_size("member")
    experts = lax.axis_size("group") * members
    rows, width = tokens.shape
    hidden_width = w_up.shape[2]
    padded = -(-(width + 3 * experts) // LANES) * LANES
    vmem = pl.BlockSpec(memory_space=pltpu.VMEM)
    hbm = pl.BlockSpec(memory_space=pl.ANY)
    dma = pltpu.SemaphoreType.DMA
    total_rows = 4 * members * rows
    return pl.pallas_call(
        functools.partial(fused_kernel, members),
        out_shape=jax.ShapeDtypeStruct((rows, width), jnp.bfloat16),
        in_specs=[vmem, vmem, vmem, vmem, hbm, hbm],
        out_specs=vmem,
        scratch_shapes=[
            pltpu.VMEM((members, 4 * rows, padded), jnp.bfloat16),
            pltpu.VMEM((hidden_width, width), jnp.bfloat16),
            pltpu.VMEM((hidden_width, width), jnp.bfloat16),
            pltpu.VMEM((members, 4 * rows, width), jnp.bfloat16),
            pltpu.VMEM((members, 2 * rows, width), jnp.bfloat16),
            pltpu.VMEM((members, rows, width), jnp.bfloat16),
            pltpu.VMEM((members, rows, width), jnp.bfloat16),
            pltpu.VMEM((members, rows, width), jnp.bfloat16),
            pltpu.VMEM((2, members, rows, width), jnp.bfloat16),
            dma((2,)),
            dma((4, members, PIECES)),
            dma((4, members, PIECES)),
            dma((2, PIECES)),
            dma((members,)),
            dma((members,)),
            dma((members, PIECES)),
            dma((members, PIECES)),
            dma((members, PIECES)),
            dma((2, members, PIECES)),
        ],
        compiler_params=pltpu.CompilerParams(
            collective_id=0, has_side_effects=True, vmem_limit_bytes=60 * 2**20
        ),
        cost_estimate=pl.CostEstimate(
            flops=4 * total_rows * width * hidden_width,
            bytes_accessed=4 * width * hidden_width,
            transcendentals=0,
        ),
    )(tokens, norm_gain, expert_ids.T, gates.T, jnp.swapaxes(w_up, 1, 2), w_down)


def routed_on_device(tokens, norm_gain, w_up, w_down, expert_ids, gates):
    groups = lax.axis_size("group")
    members = lax.axis_size("member")
    experts = groups * members
    tok_dev, picks = expert_ids.shape
    block_rows = MB_TOK
    capacity = min(block_rows, (2 * picks * block_rows + experts - 1) // experts)
    micro_count = tok_dev // block_rows
    half_width = tokens.shape[1]
    up_local = w_up[0]
    down_local = w_down[0]
    full_rows = lax.all_gather(tokens, "half", axis=1, tiled=True)
    full_float = full_rows.astype(jnp.float32)
    inverse_rms = lax.rsqrt(jnp.mean(full_float * full_float, axis=-1, keepdims=True) + epsilon)
    normed = (full_float * inverse_rms * norm_gain).astype(jnp.bfloat16)
    token_blocks = normed.reshape(micro_count, block_rows, normed.shape[1])
    id_blocks = expert_ids.reshape(micro_count, block_rows, picks)
    gate_blocks = gates.reshape(micro_count, block_rows, picks)
    row_iota = jnp.arange(block_rows, dtype=jnp.int32)
    earlier = (row_iota[:, None] > row_iota[None, :]).astype(jnp.bfloat16)

    def one_block(pieces):
        block_tokens, block_ids, weights = pieces
        expert_iota = jnp.arange(experts, dtype=jnp.int32)
        matches = block_ids[:, :, None] == expert_iota[None, None, :]
        picked = jnp.any(matches, axis=1)
        before = jnp.dot(
            earlier, picked.astype(jnp.bfloat16), preferred_element_type=jnp.float32
        ).astype(jnp.int32)
        slot_iota = jnp.arange(capacity, dtype=jnp.int32)
        slot_table = picked[:, :, None] & (before[:, :, None] == slot_iota[None, None, :])
        slot_bf = slot_table.astype(jnp.bfloat16).reshape(block_rows, experts * capacity)
        outgoing = lax.dot_general(
            slot_bf, block_tokens, (((0,), (0,)), ((), ())), preferred_element_type=jnp.float32
        )
        outgoing = outgoing.astype(jnp.bfloat16).reshape(experts, capacity, block_tokens.shape[1])
        arrived = lax.all_to_all(
            outgoing, ("group", "member"), split_axis=0, concat_axis=0, tiled=True
        )
        flat_rows = arrived.reshape(experts * capacity, arrived.shape[2])
        up_values = jnp.dot(flat_rows, up_local, preferred_element_type=jnp.float32)
        hidden = jnp.square(jax.nn.relu(up_values)).astype(jnp.bfloat16)
        partial_value = jnp.dot(hidden, down_local, preferred_element_type=jnp.float32).astype(
            jnp.bfloat16
        )
        partial_value = lax.optimization_barrier(partial_value).astype(jnp.float32)
        summed = lax.psum_scatter(
            partial_value.astype(jnp.bfloat16), "half", scatter_dimension=1, tiled=True
        )
        results = summed.reshape(experts, capacity, half_width)
        returned = lax.all_to_all(
            results, ("group", "member"), split_axis=0, concat_axis=0, tiled=True
        )
        select_table = (matches[:, :, :, None] & slot_table[:, None, :, :]).astype(jnp.bfloat16)
        select_table = select_table.reshape(block_rows, picks, experts * capacity)
        chosen_rows = jnp.einsum(
            "tks,sd->tkd",
            select_table,
            returned.reshape(experts * capacity, half_width),
            preferred_element_type=jnp.float32,
        )
        block_out = jnp.sum(weights[:, :, None] * chosen_rows, axis=1)
        return block_out.astype(jnp.bfloat16)

    outputs = lax.map(one_block, (token_blocks, id_blocks, gate_blocks))
    return outputs.reshape(tok_dev, half_width)


def solution(mesh):
    in_specs = (
        P(("parts", "group", "member"), "half"),
        P(),
        P(("group", "member"), None, "half"),
        P(("group", "member"), "half", None),
        P(("parts", "group", "member"), None),
        P(("parts", "group", "member"), None),
    )
    out_specs = P(("parts", "group", "member"), "half")
    fused = mesh.shape["half"] == 1 and mesh.shape["group"] == 4 and 1 < mesh.shape["member"] <= 4
    on_device = fused_on_device if fused else routed_on_device
    return jax.shard_map(
        on_device, mesh=mesh, in_specs=in_specs, out_specs=out_specs, check_vma=False
    )
```

```python
import functools

import jax
import jax.numpy as jnp
from jax import lax
from jax.experimental import pallas as pl
from jax.experimental.pallas import tpu as pltpu
from jax.sharding import PartitionSpec as P

MB_TOK = 32
LANES = 128
PIECES = 4

epsilon = 1e-05


def visiting_orders(members):
    middle = (members - 1) / 2
    return [
        sorted(range(members), key=lambda s: (abs(s - m), abs(s - middle)))
        for m in range(members)
    ]


def return_orders(members):
    crossing, onward = [], []
    for m, order in enumerate(visiting_orders(members)):
        crossing.append([order[1]] + [s for s in order[::-1] if s != order[1]])
        onward.append(crossing[-1] if m in (0, members - 1) else order[::-1])
    return crossing, onward


def fused_kernel(
    members,
    tok_ref,
    gain_ref,
    ids_ref,
    gates_ref,
    up_hbm,
    down_hbm,
    out_ref,
    gathered,
    up_ref,
    down_ref,
    partials,
    core_in,
    core_sum,
    x_in,
    chain_out,
    chain_in,
    w_sem,
    ag_send,
    ag_recv,
    own_send,
    core_send,
    core_recv,
    x_send,
    x_recv,
    chain_send,
    chain_recv,
):
    rows, width = tok_ref.shape
    picks = ids_ref.shape[0]
    padded = gathered.shape[2]
    piece_rows = rows // PIECES
    base = width // LANES * LANES
    off = width - base
    part = lax.axis_index("parts")
    g = lax.axis_index("group")
    m = lax.axis_index("member")
    half = lax.axis_index("half")
    experts = lax.axis_size("group") * members
    me = g * members + m
    core_peer = (part, g + 1 - 2 * lax.rem(g, 2), m, half)
    x_peer = (part, lax.rem(g + 2, 4), m, half)
    has_left = m > 0
    has_right = m < members - 1

    def chain_peer(place):
        return (part, g, place, half)

    up_copy = pltpu.make_async_copy(up_hbm.at[0], up_ref, w_sem.at[0])
    down_copy = pltpu.make_async_copy(down_hbm.at[0], down_ref, w_sem.at[1])
    up_copy.start()
    down_copy.start()

    barrier = pltpu.get_barrier_semaphore()

    def greet(peer):
        pl.semaphore_signal(barrier, inc=1, device_id=peer, device_id_type=pl.DeviceIdType.MESH)

    greet(core_peer)
    greet(x_peer)

    @pl.when(has_left)
    def _():
        greet(chain_peer(m - 1))

    @pl.when(has_right)
    def _():
        greet(chain_peer(m + 1))

    block = padded - base
    spot = lax.broadcasted_iota(jnp.int32, (block, rows), 0) - off
    kind = (spot >= experts).astype(jnp.int32) + (spot >= 2 * experts).astype(jnp.int32)
    spot_expert = spot - kind * experts
    weight = jnp.zeros((block, rows), jnp.float32)
    for k in range(picks):
        weight += jnp.where(spot_expert == ids_ref[k : k + 1, :], gates_ref[k : k + 1, :], 0.0)
    high = weight.astype(jnp.bfloat16).astype(jnp.float32)
    rest = weight - high
    middle = rest.astype(jnp.bfloat16).astype(jnp.float32)
    low = rest - middle
    pieces = jnp.where(kind == 0, high, jnp.where(kind == 1, middle, low)).T
    lane = lax.broadcasted_iota(jnp.int32, (rows, block), 1) - off
    values = tok_ref[...].astype(jnp.float32)
    inverse_rms = lax.rsqrt(jnp.mean(values * values, axis=-1, keepdims=True) + epsilon)
    normed = (values * inverse_rms * gain_ref[...].reshape(1, width)).astype(jnp.bfloat16)
    own_rows = pl.ds(0, rows)
    gathered[m, own_rows, base:padded] = jnp.zeros((rows, block), jnp.bfloat16)
    gathered[m, own_rows, 0:width] = normed
    tail = gathered[m, own_rows, base:padded].astype(jnp.float32)
    gathered[m, own_rows, base:padded] = jnp.where(lane < 0, tail, pieces).astype(jnp.bfloat16)

    pl.semaphore_wait(barrier, 2 + has_left.astype(jnp.int32) + has_right.astype(jnp.int32))

    def gather_copy(s, h, source, target, peer, send):
        return pltpu.make_async_remote_copy(
            src_ref=gathered.at[s, pl.ds(source * rows + h * piece_rows, piece_rows), :],
            dst_ref=gathered.at[s, pl.ds(target * rows + h * piece_rows, piece_rows), :],
            send_sem=send,
            recv_sem=ag_recv.at[target, s, h],
            device_id=peer,
            device_id_type=pl.DeviceIdType.MESH,
        )

    def to_chain(s, h, place):
        return gather_copy(s, h, 0, 0, chain_peer(place), ag_send.at[0, s, h])

    def to_left_first(h):
        return gather_copy(m, h, 0, 0, chain_peer(m - 1), own_send.at[0, h])

    def to_right_first(h):
        return gather_copy(m, h, 0, 0, chain_peer(m + 1), own_send.at[1, h])

    def to_x(s, h):
        return gather_copy(s, h, 0, 1, x_peer, ag_send.at[1, s, h])

    def to_core(s, h):
        return gather_copy(s, h, 0, 2, core_peer, ag_send.at[2, s, h])

    def to_core_far(s, h):
        return gather_copy(s, h, 1, 3, core_peer, ag_send.at[3, s, h])

    for h in range(PIECES):

        @pl.when(has_left)
        def _():
            to_left_first(h).start()

        @pl.when(has_right)
        def _():
            to_right_first(h).start()

        to_x(m, h).start()
        to_core(m, h).start()

    def looked_up(orders, i):
        code = m * members + i
        found = jnp.int32(0)
        for a in range(members):
            for b in range(members):
                found = found + jnp.where(code == a * members + b, orders[a][b], 0)
        return found

    orders = visiting_orders(members)
    crossing, onward_order = return_orders(members)

    def pass_on(s, h, next_place, goes_on):
        to_chain(s, h, next_place).wait_recv()

        @pl.when(goes_on)
        def _():
            to_chain(s, h, next_place).start()

        to_x(s, h).start()
        to_core(s, h).start()

    def core_copy(s, line):
        return pltpu.make_async_remote_copy(
            src_ref=partials.at[s, pl.ds((2 + line) * rows, rows), :],
            dst_ref=core_in.at[s, pl.ds(line * rows, rows), :],
            send_sem=core_send.at[s, line],
            recv_sem=core_recv.at[s, line],
            device_id=core_peer,
            device_id_type=pl.DeviceIdType.MESH,
        )

    def piece(h):
        return pl.ds(h * piece_rows, piece_rows)

    def x_copy(s, h):
        return pltpu.make_async_remote_copy(
            src_ref=core_sum.at[s, piece(h), :],
            dst_ref=x_in.at[s, piece(h), :],
            send_sem=x_send.at[s, h],
            recv_sem=x_recv.at[s, h],
            device_id=x_peer,
            device_id_type=pl.DeviceIdType.MESH,
        )

    def chain_copy(s, h, side, place):
        return pltpu.make_async_remote_copy(
            src_ref=chain_out.at[s, piece(h), :],
            dst_ref=chain_in.at[side, s, piece(h), :],
            send_sem=chain_send.at[s, h],
            recv_sem=chain_recv.at[side, s, h],
            device_id=chain_peer(place),
            device_id_type=pl.DeviceIdType.MESH,
        )

    all_lane = lax.broadcasted_iota(jnp.int32, (4 * rows, block), 1) - off
    mine = (all_lane == me) | (all_lane == me + experts) | (all_lane == me + 2 * experts)

    def add(a, b):
        return a.astype(jnp.float32) + b.astype(jnp.float32)

    def core_step(i):
        s = looked_up(crossing, i)
        core_copy(s, 1).wait_recv()
        for h in range(PIECES):
            far = pl.ds(rows + h * piece_rows, piece_rows)
            far_sum = add(partials[s, far, :], core_in[s, far, :])
            core_sum[s, piece(h), :] = far_sum.astype(jnp.bfloat16)
            x_copy(s, h).start()

    def gather_step(i, carry):
        left = m - i - 1
        right = m + i + 1
        for h in range(PIECES):

            @pl.when(left >= 0)
            def _():
                pass_on(left, h, m + 1, has_right)

            @pl.when(right < members)
            def _():
                pass_on(right, h, m - 1, has_left)

        s = looked_up(orders, i)
        @pl.when(i == members - 1)
        def _():
            core_step(0)

        for h in range(PIECES):
            to_x(s, h).wait_recv()
            to_core_far(s, h).start()

        for h in range(PIECES):
            to_core(s, h).wait_recv()
            to_core_far(s, h).wait_recv()

        @pl.when(i == 0)
        def _():
            up_copy.wait()
            down_copy.wait()

        tail_block = gathered[s, :, base:padded].astype(jnp.float32)
        row_weight = jnp.sum(jnp.where(mine, tail_block, 0.0), axis=1, keepdims=True)
        up_values = lax.dot_general(
            gathered[s, :, 0:width],
            up_ref[...],
            (((1,), (1,)), ((), ())),
            preferred_element_type=jnp.float32,
        )
        hidden = jnp.square(jnp.maximum(up_values, 0.0)).astype(jnp.bfloat16)
        down_values = jnp.dot(hidden, down_ref[...], preferred_element_type=jnp.float32)
        partials[s] = (down_values * row_weight).astype(jnp.bfloat16)
        core_copy(s, 1).start()
        core_copy(s, 0).start()
        return carry

    lax.fori_loop(0, members, gather_step, 0)

    def later_core_step(i, carry):
        core_step(i)
        return carry

    lax.fori_loop(1, members, later_core_step, 0)

    def own_sum(s, h):
        x_copy(s, h).wait_recv()
        near = add(partials[s, piece(h), :], core_in[s, piece(h), :])
        return near + x_in[s, piece(h), :].astype(jnp.float32)

    def chain_step(i, carry):
        s = looked_up(onward_order, i)
        core_copy(s, 0).wait_recv()

        def onward(side, upstream, next_place):
            for h in range(PIECES):
                total = own_sum(s, h)

                @pl.when(upstream)
                def _():
                    chain_copy(s, h, side, next_place).wait_recv()
                    arrived = chain_in[side, s, piece(h), :].astype(jnp.float32)
                    chain_out[s, piece(h), :] = (total + arrived).astype(jnp.bfloat16)

                @pl.when(jnp.logical_not(upstream))
                def _():
                    chain_out[s, piece(h), :] = total.astype(jnp.bfloat16)

                chain_copy(s, h, side, next_place).start()

        @pl.when(s > m)
        def _():
            onward(0, has_left, m + 1)

        @pl.when(s < m)
        def _():
            onward(1, has_right, m - 1)

        return carry

    lax.fori_loop(0, members - 1, chain_step, 0)
    core_copy(m, 0).wait_recv()

    for h in range(PIECES):
        total = own_sum(m, h)

        @pl.when(has_left & has_right)
        def _():
            chain_copy(m, h, 0, m + 1).wait_recv()
            chain_copy(m, h, 1, m - 1).wait_recv()
            both = add(chain_in[0, m, piece(h), :], chain_in[1, m, piece(h), :])
            out_ref[piece(h), :] = (total + both).astype(out_ref.dtype)

        @pl.when(has_left & jnp.logical_not(has_right))
        def _():
            chain_copy(m, h, 0, m - 1).wait_recv()
            one = chain_in[0, m, piece(h), :].astype(jnp.float32)
            out_ref[piece(h), :] = (total + one).astype(out_ref.dtype)

        @pl.when(has_right & jnp.logical_not(has_left))
        def _():
            chain_copy(m, h, 1, m + 1).wait_recv()
            one = chain_in[1, m, piece(h), :].astype(jnp.float32)
            out_ref[piece(h), :] = (total + one).astype(out_ref.dtype)

    for h in range(PIECES):

        @pl.when(has_left)
        def _():
            to_left_first(h).wait_send()

        @pl.when(has_right)
        def _():
            to_right_first(h).wait_send()

    def finish(s, carry):
        core_copy(s, 0).wait_send()
        core_copy(s, 1).wait_send()
        for h in range(PIECES):
            to_x(s, h).wait_send()
            to_core(s, h).wait_send()
            to_core_far(s, h).wait_send()
            x_copy(s, h).wait_send()

            @pl.when((s < m) & has_right)
            def _():
                to_chain(s, h, m + 1).wait_send()

            @pl.when((s > m) & has_left)
            def _():
                to_chain(s, h, m - 1).wait_send()

            @pl.when(s > m)
            def _():
                chain_copy(s, h, 0, m + 1).wait_send()

            @pl.when(s < m)
            def _():
                chain_copy(s, h, 1, m - 1).wait_send()

        return carry

    lax.fori_loop(0, members, finish, 0)


def fused_on_device(tokens, norm_gain, w_up, w_down, expert_ids, gates):
    members = lax.axis_size("member")
    experts = lax.axis_size("group") * members
    rows, width = tokens.shape
    hidden_width = w_up.shape[2]
    padded = -(-(width + 3 * experts) // LANES) * LANES
    vmem = pl.BlockSpec(memory_space=pltpu.VMEM)
    hbm = pl.BlockSpec(memory_space=pl.ANY)
    dma = pltpu.SemaphoreType.DMA
    total_rows = 4 * members * rows
    return pl.pallas_call(
        functools.partial(fused_kernel, members),
        out_shape=jax.ShapeDtypeStruct((rows, width), jnp.bfloat16),
        in_specs=[vmem, vmem, vmem, vmem, hbm, hbm],
        out_specs=vmem,
        scratch_shapes=[
            pltpu.VMEM((members, 4 * rows, padded), jnp.bfloat16),
            pltpu.VMEM((hidden_width, width), jnp.bfloat16),
            pltpu.VMEM((hidden_width, width), jnp.bfloat16),
            pltpu.VMEM((members, 4 * rows, width), jnp.bfloat16),
            pltpu.VMEM((members, 2 * rows, width), jnp.bfloat16),
            pltpu.VMEM((members, rows, width), jnp.bfloat16),
            pltpu.VMEM((members, rows, width), jnp.bfloat16),
            pltpu.VMEM((members, rows, width), jnp.bfloat16),
            pltpu.VMEM((2, members, rows, width), jnp.bfloat16),
            dma((2,)),
            dma((4, members, PIECES)),
            dma((4, members, PIECES)),
            dma((2, PIECES)),
            dma((members, 2)),
            dma((members, 2)),
            dma((members, PIECES)),
            dma((members, PIECES)),
            dma((members, PIECES)),
            dma((2, members, PIECES)),
        ],
        compiler_params=pltpu.CompilerParams(
            collective_id=0, has_side_effects=True, vmem_limit_bytes=60 * 2**20
        ),
        cost_estimate=pl.CostEstimate(
            flops=4 * total_rows * width * hidden_width,
            bytes_accessed=4 * width * hidden_width,
            transcendentals=0,
        ),
    )(tokens, norm_gain, expert_ids.T, gates.T, jnp.swapaxes(w_up, 1, 2), w_down)


def routed_on_device(tokens, norm_gain, w_up, w_down, expert_ids, gates):
    groups = lax.axis_size("group")
    members = lax.axis_size("member")
    experts = groups * members
    tok_dev, picks = expert_ids.shape
    block_rows = MB_TOK
    capacity = min(block_rows, (2 * picks * block_rows + experts - 1) // experts)
    micro_count = tok_dev // block_rows
    half_width = tokens.shape[1]
    up_local = w_up[0]
    down_local = w_down[0]
    full_rows = lax.all_gather(tokens, "half", axis=1, tiled=True)
    full_float = full_rows.astype(jnp.float32)
    inverse_rms = lax.rsqrt(jnp.mean(full_float * full_float, axis=-1, keepdims=True) + epsilon)
    normed = (full_float * inverse_rms * norm_gain).astype(jnp.bfloat16)
    token_blocks = normed.reshape(micro_count, block_rows, normed.shape[1])
    id_blocks = expert_ids.reshape(micro_count, block_rows, picks)
    gate_blocks = gates.reshape(micro_count, block_rows, picks)
    row_iota = jnp.arange(block_rows, dtype=jnp.int32)
    earlier = (row_iota[:, None] > row_iota[None, :]).astype(jnp.bfloat16)

    def one_block(pieces):
        block_tokens, block_ids, weights = pieces
        expert_iota = jnp.arange(experts, dtype=jnp.int32)
        matches = block_ids[:, :, None] == expert_iota[None, None, :]
        picked = jnp.any(matches, axis=1)
        before = jnp.dot(
            earlier, picked.astype(jnp.bfloat16), preferred_element_type=jnp.float32
        ).astype(jnp.int32)
        slot_iota = jnp.arange(capacity, dtype=jnp.int32)
        slot_table = picked[:, :, None] & (before[:, :, None] == slot_iota[None, None, :])
        slot_bf = slot_table.astype(jnp.bfloat16).reshape(block_rows, experts * capacity)
        outgoing = lax.dot_general(
            slot_bf, block_tokens, (((0,), (0,)), ((), ())), preferred_element_type=jnp.float32
        )
        outgoing = outgoing.astype(jnp.bfloat16).reshape(experts, capacity, block_tokens.shape[1])
        arrived = lax.all_to_all(
            outgoing, ("group", "member"), split_axis=0, concat_axis=0, tiled=True
        )
        flat_rows = arrived.reshape(experts * capacity, arrived.shape[2])
        up_values = jnp.dot(flat_rows, up_local, preferred_element_type=jnp.float32)
        hidden = jnp.square(jax.nn.relu(up_values)).astype(jnp.bfloat16)
        partial_value = jnp.dot(hidden, down_local, preferred_element_type=jnp.float32).astype(
            jnp.bfloat16
        )
        partial_value = lax.optimization_barrier(partial_value).astype(jnp.float32)
        summed = lax.psum_scatter(
            partial_value.astype(jnp.bfloat16), "half", scatter_dimension=1, tiled=True
        )
        results = summed.reshape(experts, capacity, half_width)
        returned = lax.all_to_all(
            results, ("group", "member"), split_axis=0, concat_axis=0, tiled=True
        )
        select_table = (matches[:, :, :, None] & slot_table[:, None, :, :]).astype(jnp.bfloat16)
        select_table = select_table.reshape(block_rows, picks, experts * capacity)
        chosen_rows = jnp.einsum(
            "tks,sd->tkd",
            select_table,
            returned.reshape(experts * capacity, half_width),
            preferred_element_type=jnp.float32,
        )
        block_out = jnp.sum(weights[:, :, None] * chosen_rows, axis=1)
        return block_out.astype(jnp.bfloat16)

    outputs = lax.map(one_block, (token_blocks, id_blocks, gate_blocks))
    return outputs.reshape(tok_dev, half_width)


def solution(mesh):
    in_specs = (
        P(("parts", "group", "member"), "half"),
        P(),
        P(("group", "member"), None, "half"),
        P(("group", "member"), "half", None),
        P(("parts", "group", "member"), None),
        P(("parts", "group", "member"), None),
    )
    out_specs = P(("parts", "group", "member"), "half")
    fused = mesh.shape["half"] == 1 and mesh.shape["group"] == 4 and mesh.shape["member"] == 4
    on_device = fused_on_device if fused else routed_on_device
    return jax.shard_map(
        on_device, mesh=mesh, in_specs=in_specs, out_specs=out_specs, check_vma=False
    )
```
